256 devices in a mesh: dp: 2 (over z_hi), row: 8 (over x, core), col: 16 (over z_lo, y).
Axes of the slice: x: 4, y: 4, z: 8 (z_hi: 2, z_lo: 4; z = z_hi * 4 + z_lo), core: 2. Of those that a mesh axis runs over, the one named last changes fastest.
Arguments:
- tokens: bfloat16 [8192, 6144], P(('dp', 'row'), 'col'), may hold values from -60 to 60
- layernorm_gain: float32 [6144], P('col'), may hold values from 0.1 to 1.9
- w_query: bfloat16 [6144, 6144], P('row', 'col'), may hold values from -0.078125 to 0.078125
- cotangent: bfloat16 [8192, 6144], P(('dp', 'row'), 'col'), may hold values from -2 to 2
Outputs:
- query: bfloat16 [8192, 6144], P(('dp', 'row'), 'col')
- token_gradient: bfloat16 [8192, 6144], P(('dp', 'row'), 'col')
- grad_w: float32 [6144, 6144], P('row', 'col')
The draws below stay inside these ranges and needn't reach their ends.
All inputs are finite; a program needn't handle non-finite values.
Results may differ from the reference program's by a relative error of at most 0.0049.
Values may be sent and summed in bfloat16 or wider, within the bound.
No kernel may reach another device: no remote copies, remote signals or barrier semaphores. Data moves between devices by JAX's collectives and lax.ppermute only.
A program may use at most 128 MiB of HBM per device.

```python
import math
import jax
import jax.numpy as jnp
from jax import lax

D = 6144
TOKENS = 8192


def draw_tokens(key, part):
    key = jax.random.fold_in(key, 11)
    first_moment_term, second_moment_term, third = jax.random.split(key, 3)
    row_scale = jnp.exp(jax.random.uniform(second_moment_term, (TOKENS, 1), jnp.float32, math.log(0.1), 0.0))
    ramp = 1.0 + 2.0 * jnp.arange(D, dtype=jnp.float32) / (D - 1)
    col_scale = ramp * jnp.exp(jax.random.uniform(third, (D,), jnp.float32, 0.0, math.log(3.0)))
    noise = jnp.clip(jax.random.normal(first_moment_term, (TOKENS, D), jnp.float32), -6.0, 6.0)
    values = noise * col_scale[None, :] * row_scale
    return values.astype(jnp.bfloat16)


def block_levels(key, shape, cuts, low, top_value):
    def one(dim, shards_of):
        steps = jax.random.uniform(jax.random.fold_in(jax.random.fold_in(key, 6), dim), (shards_of,), jnp.float32, low / len(cuts), top_value / len(cuts))
        return jnp.repeat(jnp.exp(steps), shape[dim] // shards_of).reshape((-1,) + (1,) * (len(shape) - dim - 1))

    loudness = one(*cuts[0])
    for cut in cuts[1:]:
        loudness = loudness * one(*cut)
    return loudness


def gaussian(stream_key, shape, width, bound, cuts=(), kind=jnp.bfloat16):
    array = jax.random.normal(stream_key, shape, jnp.float32) * width
    if len(cuts) > 0:
        array = block_levels(stream_key, shape, cuts, -0.22, 0.18) * array
    return jnp.clip(array, min=-bound, max=bound).astype(kind)


def setup_inputs(seed: int = 0) -> dict:
    key_list = jax.random.split(jax.random.key(seed), 5)
    return {
        "tokens": draw_tokens(jax.random.fold_in(key_list[4], 71), 0),
        "layernorm_gain": jnp.clip(1.0 + 0.18 * jax.random.normal(key_list[1], (D,), jnp.float32), 0.1, 1.9),
        "w_query": gaussian(key_list[2], (D, D), D ** -0.5, 0.078125, ((0, 8), (1, 16))),
        "cotangent": gaussian(key_list[3], (TOKENS, D), 0.125, 2.0, ((0, 16), (1, 16))),
    }


def reference(tokens, layernorm_gain, w_query, cotangent):
    values = tokens.astype(jnp.float32)
    mean_x = lax.optimization_barrier(jnp.mean(values, axis=1, keepdims=True))
    centered_input = values - mean_x
    var_x = lax.optimization_barrier(jnp.mean(centered_input * centered_input, axis=1, keepdims=True))
    inverse_deviation = lax.rsqrt(var_x + 1e-06)
    standardized_input = centered_input * inverse_deviation
    normed_tokens = (standardized_input * layernorm_gain[None, :]).astype(jnp.bfloat16)
    query = jnp.dot(normed_tokens, w_query, preferred_element_type=jnp.float32).astype(jnp.bfloat16)
    grad_normed = jnp.dot(cotangent, w_query.T, preferred_element_type=jnp.float32)
    gradient_standardized = grad_normed * layernorm_gain[None, :]
    first_moment_term = lax.optimization_barrier(jnp.mean(gradient_standardized, axis=1, keepdims=True))
    second_moment_term = lax.optimization_barrier(jnp.mean(gradient_standardized * standardized_input, axis=1, keepdims=True))
    token_gradient = ((gradient_standardized - first_moment_term - standardized_input * second_moment_term) * inverse_deviation).astype(jnp.bfloat16)
    grad_w = jnp.dot(normed_tokens.T, cotangent, preferred_element_type=jnp.float32)
    return (query, token_gradient, grad_w)
```

```python
import itertools

import jax
import jax.numpy as jnp
from jax import lax
from jax.experimental import pallas as pl
from jax.experimental.pallas import tpu as pltpu
from jax.sharding import Mesh, PartitionSpec as P

AXES = ("dp", "x", "c", "z", "y")
SIZES = dict(dp=2, x=4, c=2, z=4, y=4)
T = 512
F = 384
VMEM_LIMIT = 40 * 1024 * 1024
F32 = jnp.float32
BF16 = jnp.bfloat16


def send(value, axes, to):
    coords = list(itertools.product(*(range(SIZES[a]) for a in axes)))
    flat = {c: i for i, c in enumerate(coords)}
    perm = [(flat[c], flat[tuple(to(*c))]) for c in coords]
    return lax.ppermute(value, axes if len(axes) > 1 else axes[0], perm)


def swap(value, axis, e):
    return send(value, (axis,), lambda i: (i ^ e,))


def dot_nt(a, b):
    return lax.dot_general(a, b, (((1,), (1,)), ((), ())), preferred_element_type=F32)


def dot_nn(a, b):
    return lax.dot_general(a, b, (((1,), (0,)), ((), ())), preferred_element_type=F32)


def load_all(copies):
    for c in copies:
        c.start()


def lanes(e, width=F):
    return pl.ds(e * width, width)


def call(kernel, out_shape, scratch, flops, nbytes, n_any, n_vmem):
    def outer(*args):
        return pl.pallas_call(
            kernel,
            out_shape=out_shape,
            in_specs=[pl.BlockSpec(memory_space=pl.ANY)] * n_any
            + [pl.BlockSpec(memory_space=pltpu.VMEM)] * n_vmem,
            out_specs=jax.tree.map(lambda _: pl.BlockSpec(memory_space=pltpu.VMEM), out_shape),
            scratch_shapes=scratch,
            compiler_params=pltpu.CompilerParams(vmem_limit_bytes=VMEM_LIMIT),
            cost_estimate=pl.CostEstimate(flops=flops, bytes_accessed=nbytes, transcendentals=0),
        )(*args)

    return outer


def gw_other_kernel(*refs):
    normed, cots = refs[0:4], refs[4:8]
    outs, turned = refs[8:12], refs[12]
    nbuf, cbuf, sems = refs[13:]
    x, c, z = lax.axis_index("x"), lax.axis_index("c"), lax.axis_index("z")
    copies = [pltpu.make_async_copy(normed[e], nbuf.at[z ^ e], sems.at[e]) for e in range(4)]
    copies += [
        pltpu.make_async_copy(cots[e], cbuf.at[e // 2, :, lanes(e % 2)], sems.at[4 + e])
        for e in range(4)
    ]
    load_all(copies)
    for cp in copies:
        cp.wait()
    for e in range(4):
        row = x ^ e
        nt = nbuf[row].T
        turned[e] = nt
        outs[e][...] = dot_nn(nt, cbuf[1 - c]).astype(BF16)


def gw_own_kernel(*refs):
    turned, cots, other = refs[0], refs[1:5], refs[5:9]
    outs = refs[9:13]
    tbuf, cbuf, obuf, sems = refs[13:]
    c = lax.axis_index("c")
    copies = [pltpu.make_async_copy(turned, tbuf, sems.at[0])]
    copies += [
        pltpu.make_async_copy(cots[e], cbuf.at[e // 2, :, lanes(e % 2)], sems.at[1 + e])
        for e in range(4)
    ]
    copies += [pltpu.make_async_copy(other[e], obuf.at[e], sems.at[5 + e]) for e in range(4)]
    load_all(copies)
    for cp in copies:
        cp.wait()
    for e in range(4):
        total = dot_nn(tbuf[e], cbuf[c]) + obuf[e].astype(F32)
        outs[e][...] = total.astype(outs[e].dtype)


def weight_copies(mine, theirs, wbuf, sems, first, x, c):
    copies = []
    for e in range(4):
        copies.append(pltpu.make_async_copy(mine[e], wbuf.at[x ^ e, c], sems.at[first + 2 * e]))
        copies.append(
            pltpu.make_async_copy(theirs[e], wbuf.at[x ^ e, 1 - c], sems.at[first + 2 * e + 1])
        )
    return copies


def back_kernel(*refs):
    mine, theirs, cots, normed = refs[0:4], refs[4:8], refs[8:12], refs[12:16]
    gains = refs[16]
    outs, sums = refs[17:21], refs[21]
    wbuf, cbuf, nbuf, sems = refs[22:]
    x, c, z = lax.axis_index("x"), lax.axis_index("c"), lax.axis_index("z")
    copies = weight_copies(mine, theirs, wbuf, sems, 0, x, c)
    copies += [
        pltpu.make_async_copy(cots[e], cbuf.at[e // 2, :, lanes(e % 2)], sems.at[8 + e])
        for e in range(4)
    ]
    copies += [pltpu.make_async_copy(normed[e], nbuf.at[e], sems.at[12 + e]) for e in range(4)]
    load_all(copies)
    for cp in copies:
        cp.wait()
    first = jnp.zeros((T, 1), F32)
    second = jnp.zeros((T, 1), F32)
    for e in (3, 2, 1, 0):
        rows = z ^ e
        part = dot_nt(cbuf[0], wbuf[rows, 0]) + dot_nt(cbuf[1], wbuf[rows, 1])
        first = first + jnp.sum(part * gains[e : e + 1, :], axis=1, keepdims=True)
        second = second + jnp.sum(part * nbuf[e].astype(F32), axis=1, keepdims=True)
        outs[e][...] = part.astype(outs[e].dtype)
    lane = lax.broadcasted_iota(jnp.int32, (T, 128), 1)
    both = jnp.where(lane == 0, first, second)
    sums[...] = both.T[:8]


def query_kernel(*refs):
    mine, theirs, normed = refs[0:4], refs[4:8], refs[8:12]
    outs = refs[12:16]
    wbuf, nbuf, sems = refs[16:]
    x, c, z = lax.axis_index("x"), lax.axis_index("c"), lax.axis_index("z")
    copies = weight_copies(mine, theirs, wbuf, sems, 0, x, c)
    copies += [pltpu.make_async_copy(normed[e], nbuf.at[z ^ e], sems.at[8 + e]) for e in range(4)]
    load_all(copies)
    for cp in copies:
        cp.wait()
    for half in (1, 0):
        part = dot_nn(nbuf[0], wbuf[0, half])
        for k in range(1, 4):
            part = part + dot_nn(nbuf[k], wbuf[k, half])
        for a in range(2):
            out = outs[2 * half + a]
            out[...] = part[:, a * F : (a + 1) * F].astype(out.dtype)


def shape(*dims, dtype=BF16):
    return jax.ShapeDtypeStruct(dims, dtype)


def merge(means, squares, count):
    mean = sum(means) / len(means)
    spread = sum((m - mean) * (m - mean) for m in means)
    return mean, sum(squares) + count * spread


def on_device(tokens, gain, w, cot):
    c, z, y = lax.axis_index("c"), lax.axis_index("z"), lax.axis_index("y")
    odd = y % 2

    def to_a(s, yy):
        return ((yy >> 1) ^ s, 2 * s + (yy & 1))

    def to_b(s, yy):
        return ((yy >> 1) ^ s, 2 * s + 1 - (yy & 1))

    wa = send(lax.dynamic_slice(w, (odd * F, 0), (F, F)), ("c", "y"), to_a)
    wb = send(lax.dynamic_slice(w, ((1 - odd) * F, 0), (F, F)), ("c", "y"), to_b)
    w_mine = [jnp.concatenate([wa, wb], axis=1)]
    w_mine += [swap(w_mine[0], "x", e) for e in (1, 2, 3)]
    w_theirs = [swap(m, "c", 1) for m in w_mine]

    tok = [tokens] + [swap(tokens, "z", e) for e in (1, 2, 3)]
    cots = [cot] + [swap(cot, "y", e) for e in (1, 2, 3)]

    values = tokens.astype(F32)
    own_mean = jnp.sum(values, axis=1) / F
    centred = values - own_mean[:, None]
    own = jnp.stack([own_mean, jnp.sum(centred * centred, axis=1)])
    parts = [own] + [swap(own, "y", e) for e in (1, 2, 3)]
    mean_y, squares_y = merge([p[0] for p in parts], [p[1] for p in parts], F)
    packet = jnp.concatenate([mean_y, squares_y, gain])
    packets = [packet] + [swap(packet, "z", e) for e in (1, 2, 3)]
    mean, squares = merge([p[:T] for p in packets], [p[T : 2 * T] for p in packets], 4 * F)
    gains = [p[2 * T :] for p in packets]
    width = 16 * F
    inverse = lax.rsqrt(squares / width + 1e-06)[:, None]
    mean = mean[:, None]

    def standardize(block):
        return (block.astype(F32) - mean) * inverse

    normed = [(standardize(b) * g[None, :]).astype(BF16) for b, g in zip(tok, gains)]

    dma = pltpu.SemaphoreType.DMA
    gw = call(
        gw_other_kernel,
        [shape(F, 2 * F)] * 4 + [shape(4, F, T)],
        [pltpu.VMEM((4, T, F), BF16), pltpu.VMEM((2, T, 2 * F), BF16), dma((8,))],
        2 * T * 4 * F * 2 * F,
        7_000_000,
        8,
        0,
    )(*normed, *cots)
    turned = gw[4]
    gw_theirs = [swap(g, "c", 1) for g in gw[:4]]

    back = call(
        back_kernel,
        [shape(T, F, dtype=F32)] + [shape(T, F)] * 3 + [shape(8, T, dtype=F32)],
        [
            pltpu.VMEM((4, 2, F, 2 * F), BF16),
            pltpu.VMEM((2, T, 2 * F), BF16),
            pltpu.VMEM((4, T, F), BF16),
            dma((16,)),
        ],
        2 * T * 4 * F * 4 * F,
        12_000_000,
        16,
        1,
    )(*w_mine, *w_theirs, *cots, *normed, jnp.stack(gains))
    grad_parts = [back[0]] + [swap(back[e], "z", e) for e in (1, 2, 3)]

    gw_sum = call(
        gw_own_kernel,
        [shape(F, 2 * F, dtype=F32)] + [shape(F, 2 * F)] * 3,
        [
            pltpu.VMEM((4, F, T), BF16),
            pltpu.VMEM((2, T, 2 * F), BF16),
            pltpu.VMEM((4, F, 2 * F), BF16),
            dma((9,)),
        ],
        2 * T * 4 * F * 2 * F,
        9_000_000,
        9,
        0,
    )(turned, *cots, *gw_theirs)
    gw_parts = [gw_sum[0]] + [swap(gw_sum[e], "x", e) for e in (1, 2, 3)]

    query_out = call(
        query_kernel,
        [shape(T, F, dtype=F32)] + [shape(T, F)] * 3,
        [pltpu.VMEM((4, 2, F, 2 * F), BF16), pltpu.VMEM((4, T, F), BF16), dma((12,))],
        2 * T * 4 * F * 4 * F,
        9_000_000,
        12,
        0,
    )(*w_mine, *w_theirs, *normed)
    query_parts = [query_out[0]] + [swap(query_out[e], "y", e) for e in (1, 2, 3)]

    block = sum(p.astype(F32) for p in gw_parts).astype(BF16)

    def home(a):
        return lambda d, cc, yy: (d, yy >> 1, yy ^ (2 * cc + a))

    def away(a):
        return lambda d, cc, yy: (1 - d, yy >> 1, yy ^ (2 * cc + a))

    halves = [block[:, :F], block[:, F:]]
    far = [send(halves[a], ("dp", "c", "y"), away(a)) for a in (0, 1)]
    near = [send(halves[a], ("dp", "c", "y"), home(a)) for a in (0, 1)]
    got_a, got_b = (n.astype(F32) + f.astype(F32) for n, f in zip(near, far))
    even = odd == 0
    grad_w = jnp.concatenate([jnp.where(even, got_a, got_b), jnp.where(even, got_b, got_a)])

    sums = back[4][:2]
    sums = sums + sum(swap(sums, "y", e) for e in (1, 2, 3))
    sums = sums + sum(swap(sums, "z", e) for e in (1, 2, 3))
    first, second = sums[0][:, None] / width, sums[1][:, None] / width
    grad_hat = sum(p.astype(F32) for p in grad_parts) * gain[None, :]
    token_gradient = ((grad_hat - first - standardize(tokens) * second) * inverse).astype(BF16)
    query = sum(p.astype(F32) for p in query_parts).astype(BF16)
    return query, token_gradient, grad_w


def solution(mesh):
    fine = Mesh(mesh.devices.reshape([SIZES[a] for a in AXES]), AXES)
    rows, cols = ("dp", "x", "c"), ("z", "y")
    in_specs = (P(rows, cols), P(cols), P(("x", "c"), cols), P(rows, cols))
    out_specs = (P(rows, cols), P(rows, cols), P(("x", "c"), cols))
    return jax.shard_map(
        on_device, mesh=fine, in_specs=in_specs, out_specs=out_specs, check_vma=False
    )
```

```python
import itertools

import jax
import jax.numpy as jnp
from jax import lax
from jax.experimental import pallas as pl
from jax.experimental.pallas import tpu as pltpu
from jax.sharding import Mesh, PartitionSpec as P

AXES = ("dp", "x", "c", "z", "y")
SIZES = dict(dp=2, x=4, c=2, z=4, y=4)
T = 512
F = 384
VMEM_LIMIT = 60 * 1024 * 1024
F32 = jnp.float32
BF16 = jnp.bfloat16


def send(value, axes, to):
    coords = list(itertools.product(*(range(SIZES[a]) for a in axes)))
    flat = {c: i for i, c in enumerate(coords)}
    perm = [(flat[c], flat[tuple(to(*c))]) for c in coords]
    return lax.ppermute(value, axes if len(axes) > 1 else axes[0], perm)


def swap(value, axis, e):
    return send(value, (axis,), lambda i: (i ^ e,))


def dot_nt(a, b):
    return lax.dot_general(a, b, (((1,), (1,)), ((), ())), preferred_element_type=F32)


def dot_nn(a, b):
    return lax.dot_general(a, b, (((1,), (0,)), ((), ())), preferred_element_type=F32)


def load_all(copies):
    for c in copies:
        c.start()


def lanes(e, width=F):
    return pl.ds(e * width, width)


def call(kernel, out_shape, scratch, cost, n_any, n_vmem):
    def outer(*args):
        return pl.pallas_call(
            kernel,
            out_shape=out_shape,
            in_specs=[pl.BlockSpec(memory_space=pl.ANY)] * n_any
            + [pl.BlockSpec(memory_space=pltpu.VMEM)] * n_vmem,
            out_specs=jax.tree.map(lambda _: pl.BlockSpec(memory_space=pltpu.VMEM), out_shape),
            scratch_shapes=scratch,
            compiler_params=pltpu.CompilerParams(vmem_limit_bytes=VMEM_LIMIT),
            cost_estimate=pl.CostEstimate(flops=cost, bytes_accessed=cost, transcendentals=0),
        )(*args)

    return outer


def cot_copies(cots, cbuf, sems, first):
    y = lax.axis_index("y")
    return [
        pltpu.make_async_copy(cots.at[y ^ e], cbuf.at[e // 2, :, lanes(e % 2)], sems.at[first + e])
        for e in range(4)
    ]


def gw_other_kernel(*refs):
    normed, cots = refs[0:4], refs[4]
    outs, turned = refs[5:9], refs[9]
    nbuf, cbuf, sems = refs[10:]
    x, c, z = lax.axis_index("x"), lax.axis_index("c"), lax.axis_index("z")
    copies = [pltpu.make_async_copy(normed[e], nbuf.at[z ^ e], sems.at[e]) for e in range(4)]
    copies += cot_copies(cots, cbuf, sems, 4)
    load_all(copies)
    for cp in copies:
        cp.wait()
    for e in range(4):
        row = x ^ e
        nt = nbuf[row].T
        turned[e] = nt
        outs[e][...] = dot_nn(nt, cbuf[1 - c]).astype(BF16)


def gw_own_kernel(*refs):
    turned, cots, other = refs[0], refs[1], refs[2:6]
    outs = refs[6:10]
    tbuf, cbuf, obuf, sems = refs[10:]
    c = lax.axis_index("c")
    copies = [pltpu.make_async_copy(turned, tbuf, sems.at[0])]
    copies += cot_copies(cots, cbuf, sems, 1)
    copies += [pltpu.make_async_copy(other[e], obuf.at[e], sems.at[5 + e]) for e in range(4)]
    load_all(copies)
    for cp in copies:
        cp.wait()
    for e in range(4):
        total = dot_nn(tbuf[e], cbuf[c]) + obuf[e].astype(F32)
        outs[e][...] = total.astype(outs[e].dtype)


def weight_copies(mine, theirs, wbuf, sems, first, x, c):
    copies = []
    for e in range(4):
        copies.append(pltpu.make_async_copy(mine[e], wbuf.at[x ^ e, c], sems.at[first + 2 * e]))
        copies.append(
            pltpu.make_async_copy(theirs[e], wbuf.at[x ^ e, 1 - c], sems.at[first + 2 * e + 1])
        )
    return copies


def back_kernel(*refs):
    mine, theirs, cots = refs[0:4], refs[4:8], refs[8]
    outs = refs[9:13]
    wbuf, cbuf, sems = refs[13:]
    x, c, z = lax.axis_index("x"), lax.axis_index("c"), lax.axis_index("z")
    copies = weight_copies(mine, theirs, wbuf, sems, 0, x, c)
    copies += cot_copies(cots, cbuf, sems, 8)
    load_all(copies)
    for cp in copies:
        cp.wait()
    for e in (3, 2, 1, 0):
        rows = z ^ e
        part = dot_nt(cbuf[0], wbuf[rows, 0]) + dot_nt(cbuf[1], wbuf[rows, 1])
        outs[e][...] = part.astype(outs[e].dtype)


def sums_kernel(*refs):
    parts, normed, gains, sums = refs[0:4], refs[4:8], refs[8], refs[9]
    first = jnp.zeros((T, 1), F32)
    second = jnp.zeros((T, 1), F32)
    for e in range(4):
        part = parts[e][...].astype(F32)
        first = first + jnp.sum(part * gains[e : e + 1, :], axis=1, keepdims=True)
        second = second + jnp.sum(part * normed[e][...].astype(F32), axis=1, keepdims=True)
    lane = lax.broadcasted_iota(jnp.int32, (T, 128), 1)
    both = jnp.where(lane == 0, first, second)
    sums[...] = both.T[:8]


def query_kernel(*refs):
    mine, theirs, normed = refs[0:4], refs[4:8], refs[8:12]
    out = refs[12]
    wbuf, nbuf, sems = refs[13:]
    x, c, z, y = (lax.axis_index(a) for a in "xczy")
    copies = weight_copies(mine, theirs, wbuf, sems, 0, x, c)
    copies += [pltpu.make_async_copy(normed[e], nbuf.at[z ^ e], sems.at[8 + e]) for e in range(4)]
    load_all(copies)
    for cp in copies:
        cp.wait()
    for half in range(2):
        part = dot_nn(nbuf[0], wbuf[0, half])
        for k in range(1, 4):
            part = part + dot_nn(nbuf[k], wbuf[k, half])
        for a in range(2):
            out[y ^ (2 * half + a)] = part[:, a * F : (a + 1) * F].astype(BF16)


def shape(*dims, dtype=BF16):
    return jax.ShapeDtypeStruct(dims, dtype)


def after(value, dep):
    return lax.optimization_barrier((value, dep))


def merge(a, b, count):
    gap = a[0] - b[0]
    return jnp.stack([0.5 * (a[0] + b[0]), a[1] + b[1] + (0.5 * count) * gap * gap])


def on_device(tokens, gain, w, cot):
    z, y = lax.axis_index("z"), lax.axis_index("y")
    odd = y % 2

    def to_a(s, yy):
        return ((yy >> 1) ^ s, 2 * s + (yy & 1))

    def to_b(s, yy):
        return ((yy >> 1) ^ s, 2 * s + 1 - (yy & 1))

    wa = send(lax.dynamic_slice(w, (odd * F, 0), (F, F)), ("c", "y"), to_a)
    wb = send(lax.dynamic_slice(w, ((1 - odd) * F, 0), (F, F)), ("c", "y"), to_b)
    values = tokens.astype(F32)
    own_mean = jnp.sum(values, axis=1) / F
    centred = values - own_mean[:, None]
    stat = jnp.stack([own_mean, jnp.sum(centred * centred, axis=1)])
    stat = merge(stat, swap(stat, "y", 1), F)
    stat = merge(stat, swap(stat, "y", 2), 2 * F)

    tok1, tok2 = swap(tokens, "z", 1), swap(tokens, "z", 2)
    tok = [tokens, tok1, tok2, swap(tok2, "z", 1)]

    cot, wa, wb, stat = lax.optimization_barrier((cot, wa, wb, stat))
    cots = lax.all_to_all(jnp.broadcast_to(cot, (4, T, F)), "y", 0, 0, tiled=True)

    w0 = jnp.concatenate([wa, wb], axis=1)
    w1 = swap(w0, "x", 1)
    w3 = swap(w0, "x", 3)
    w_mine = [w0, w1, swap(w0, "x", 2), w3]
    w_theirs = [swap(m, "c", 1) for m in w_mine]

    packet = jnp.concatenate([stat.reshape(-1), gain])
    other = swap(packet, "z", 1)
    stat = merge(stat, other[: 2 * T].reshape(2, T), 4 * F)
    packet = jnp.concatenate([stat.reshape(-1), gain, other[2 * T :]])
    other2 = swap(packet, "z", 2)
    stat = merge(stat, other2[: 2 * T].reshape(2, T), 8 * F)
    gains = [gain, other[2 * T :], other2[2 * T : 2 * T + F], other2[2 * T + F :]]

    width = 16 * F
    inverse = lax.rsqrt(stat[1] / width + 1e-06)[:, None]
    mean = stat[0][:, None]

    def standardize(block):
        return (block.astype(F32) - mean) * inverse

    normed = [(standardize(b) * g[None, :]).astype(BF16) for b, g in zip(tok, gains)]

    dma = pltpu.SemaphoreType.DMA
    gw = call(
        gw_other_kernel,
        [shape(F, 2 * F)] * 4 + [shape(4, F, T)],
        [pltpu.VMEM((4, T, F), BF16), pltpu.VMEM((2, T, 2 * F), BF16), dma((8,))],
        1,
        5,
        0,
    )(*normed, cots)
    turned = gw[4]
    gw_theirs = [swap(g, "c", 1) for g in gw[:4]]

    w_theirs, turned = after(w_theirs, turned)
    back = call(
        back_kernel,
        [shape(T, F, dtype=F32)] + [shape(T, F)] * 3,
        [pltpu.VMEM((4, 2, F, 2 * F), BF16), pltpu.VMEM((2, T, 2 * F), BF16), dma((12,))],
        40_000_000,
        9,
        0,
    )(*w_mine, *w_theirs, cots)
    turned, back = after(turned, back)
    gw_sum = call(
        gw_own_kernel,
        [shape(F, 2 * F, dtype=F32)] + [shape(F, 2 * F)] * 3,
        [
            pltpu.VMEM((4, F, T), BF16),
            pltpu.VMEM((2, T, 2 * F), BF16),
            pltpu.VMEM((4, F, 2 * F), BF16),
            dma((9,)),
        ],
        1,
        6,
        0,
    )(turned, cots, *gw_theirs)
    relay = swap(back[3], "z", 1)
    grad1 = swap(back[1], "z", 1)
    relay, gw_sum = after(relay, gw_sum)
    message = (back[2].astype(F32) + relay.astype(F32)).astype(BF16)
    normed, message, gw_sum = lax.optimization_barrier((normed, message, gw_sum))
    grad2 = swap(message, "z", 2)
    grad_parts = [back[0], grad1, grad2]

    gw_parts = [gw_sum[0]] + [swap(gw_sum[e], "x", e) for e in (1, 2, 3)]

    sums = call(sums_kernel, shape(8, T, dtype=F32), [], 1, 0, 9)(
        *back, *normed, jnp.stack(gains)
    )[:2]
    sums = lax.all_to_all(jnp.broadcast_to(sums, (16, 2, T)), ("z", "y"), 0, 0, tiled=True)
    sums = jnp.sum(sums, axis=0)

    query_out = call(
        query_kernel,
        shape(4, T, F),
        [pltpu.VMEM((4, 2, F, 2 * F), BF16), pltpu.VMEM((4, T, F), BF16), dma((12,))],
        1,
        12,
        0,
    )(*w_mine, *w_theirs, *normed)
    block = sum(p.astype(F32) for p in gw_parts).astype(BF16)

    def home(a):
        return lambda d, cc, yy: (d, yy >> 1, yy ^ (2 * cc + a))

    def away(a):
        return lambda d, cc, yy: (1 - d, yy >> 1, yy ^ (2 * cc + a))

    block, grad_parts, sums, query_out = lax.optimization_barrier((block, grad_parts, sums, query_out))
    halves = [block[:, :F], block[:, F:]]
    far = [send(halves[a], ("dp", "c", "y"), away(a)) for a in (0, 1)]
    near = [send(halves[a], ("dp", "c", "y"), home(a)) for a in (0, 1)]

    query_parts = lax.all_to_all(query_out, "y", 0, 0, tiled=True)

    got_a, got_b = (n.astype(F32) + f.astype(F32) for n, f in zip(near, far))
    even = odd == 0
    grad_w = jnp.concatenate([jnp.where(even, got_a, got_b), jnp.where(even, got_b, got_a)])

    first, second = sums[0][:, None] / width, sums[1][:, None] / width
    grad_hat = sum(p.astype(F32) for p in grad_parts) * gain[None, :]
    token_gradient = ((grad_hat - first - standardize(tokens) * second) * inverse).astype(BF16)
    query = jnp.sum(query_parts.astype(F32), axis=0).astype(BF16)
    return query, token_gradient, grad_w


def solution(mesh):
    fine = Mesh(mesh.devices.reshape([SIZES[a] for a in AXES]), AXES)
    rows, cols = ("dp", "x", "c"), ("z", "y")
    in_specs = (P(rows, cols), P(cols), P(("x", "c"), cols), P(rows, cols))
    out_specs = (P(rows, cols), P(rows, cols), P(("x", "c"), cols))
    return jax.shard_map(
        on_device, mesh=fine, in_specs=in_specs, out_specs=out_specs, check_vma=False
    )
```

```python
import functools
import itertools

import jax
import jax.numpy as jnp
from jax import lax
from jax.experimental import pallas as pl
from jax.experimental.pallas import tpu as pltpu
from jax.sharding import Mesh, PartitionSpec as P

AXES = ("dp", "x", "c", "z", "y")
SIZES = dict(dp=2, x=4, c=2, z=4, y=4)
T = 512
F = 384
MIB = 1024 * 1024
F32 = jnp.float32
BF16 = jnp.bfloat16


def send(value, axes, to):
    coords = list(itertools.product(*(range(SIZES[a]) for a in axes)))
    flat = {c: i for i, c in enumerate(coords)}
    perm = [(flat[c], flat[tuple(to(*c))]) for c in coords]
    return lax.ppermute(value, axes if len(axes) > 1 else axes[0], perm)


def swap(value, axis, e):
    return send(value, (axis,), lambda i: (i ^ e,))


def dot_nt(a, b):
    return lax.dot_general(a, b, (((1,), (1,)), ((), ())), preferred_element_type=F32)


def dot_nn(a, b):
    return lax.dot_general(a, b, (((1,), (0,)), ((), ())), preferred_element_type=F32)


def load_all(copies):
    for c in copies:
        c.start()


def lanes(e, width=F):
    return pl.ds(e * width, width)


def call(kernel, out_shape, scratch, cost, n_any, n_vmem, limit=10):
    def outer(*args):
        return pl.pallas_call(
            kernel,
            out_shape=out_shape,
            in_specs=[pl.BlockSpec(memory_space=pl.ANY)] * n_any
            + [pl.BlockSpec(memory_space=pltpu.VMEM)] * n_vmem,
            out_specs=jax.tree.map(lambda _: pl.BlockSpec(memory_space=pltpu.VMEM), out_shape),
            scratch_shapes=scratch,
            compiler_params=pltpu.CompilerParams(vmem_limit_bytes=limit * MIB),
            cost_estimate=pl.CostEstimate(flops=cost, bytes_accessed=cost, transcendentals=0),
        )(*args)

    return outer


def cot_copies(cots, cbuf, sems, first):
    y = lax.axis_index("y")
    return [
        pltpu.make_async_copy(cots.at[y ^ e], cbuf.at[e // 2, :, lanes(e % 2)], sems.at[first + e])
        for e in range(4)
    ]


def gw_other_kernel(*refs):
    normed, cots = refs[0:4], refs[4]
    out, turned = refs[5:7]
    nbuf, cbuf, sems = refs[7:]
    x, c, z = lax.axis_index("x"), lax.axis_index("c"), lax.axis_index("z")
    copies = [pltpu.make_async_copy(normed[e], nbuf.at[z ^ e], sems.at[e]) for e in range(4)]
    copies += cot_copies(cots, cbuf, sems, 4)
    load_all(copies)
    for cp in copies:
        cp.wait()
    for e in range(4):
        row = x ^ e
        nt = nbuf[row].T
        turned[e] = nt
        out[e] = dot_nn(nt, cbuf[1 - c]).astype(BF16)


def gw_own_kernel(*refs):
    cots, turned, other = refs[0:3]
    outs = refs[3:7]
    cbuf, sems = refs[7:]
    c, y = lax.axis_index("c"), lax.axis_index("y")
    copies = [
        pltpu.make_async_copy(cots.at[y ^ (2 * c + a)], cbuf.at[:, lanes(a)], sems.at[a])
        for a in range(2)
    ]
    load_all(copies)
    for cp in copies:
        cp.wait()
    for e in range(4):
        total = dot_nn(turned[e], cbuf[...]) + other[e].astype(F32)
        outs[e][...] = total.astype(outs[e].dtype)


def weight_copies(mine, theirs, wbuf, sems):
    x, c = lax.axis_index("x"), lax.axis_index("c")
    copies = []
    for e in range(4):
        rows = pl.ds(pl.multiple_of((x ^ e) * F, F), F)
        for half, part in ((c, mine[e]), (1 - c, theirs[e])):
            columns = pl.ds(pl.multiple_of(half * 2 * F, 2 * F), 2 * F)
            copies.append(
                pltpu.make_async_copy(part, wbuf.at[rows, columns], sems.at[x ^ e, half])
            )
    return copies


def write_rows(rows, sums):
    hi = sums.astype(BF16)
    rest = sums - hi.astype(F32)
    mid = rest.astype(BF16)
    low = (rest - mid.astype(F32)).astype(BF16)
    parts = jnp.concatenate([hi.astype(F32), mid.astype(F32), low.astype(F32)])
    tail = jnp.concatenate([parts[:, F:], jnp.zeros((6, 2 * F - T), F32)], axis=1)
    rows[...] = jnp.concatenate([parts[:, :F], tail, jnp.zeros((4, F), F32)]).astype(BF16)


def read_rows(rows):
    rows = rows.astype(F32)
    parts = jnp.concatenate([rows[:6], rows[6:12, : T - F]], axis=1)
    return parts[0:2] + parts[2:4] + parts[4:6]


def message_kernel(share, relay, sums, out, total):
    out[:T] = (share[...].astype(F32) + relay[:T].astype(F32)).astype(BF16)
    total[...] = sums[0:2] + read_rows(relay[T:])
    write_rows(out.at[T:], total[...])


def products_kernel(*refs):
    mine, theirs, cots, normed, gains = refs[0:4], refs[4:8], refs[8], refs[9:13], refs[13]
    outs, query, sums = refs[14:18], refs[18], refs[19]
    wbuf, cbuf, nbuf, wsems, csems, nsems = refs[20:]
    y, z = lax.axis_index("y"), lax.axis_index("z")
    columns = [
        pltpu.make_async_copy(cots.at[y ^ e], cbuf.at[:, lanes(e)], csems.at[e]) for e in range(4)
    ]
    load_all(columns)
    load_all(weight_copies(mine, theirs, wbuf, wsems))
    own = [pl.ds(pl.multiple_of((z ^ e) * F, F), F) for e in range(4)]
    features = [
        pltpu.make_async_copy(normed[e], nbuf.at[:, own[e]], nsems.at[e]) for e in range(4)
    ]
    load_all(features)
    for cp in columns + features:
        cp.wait()
    first = jnp.zeros((T, 1), F32)
    second = jnp.zeros((T, 1), F32)
    for e in (3, 2, 1, 0):
        for half in range(2):
            arrived = wbuf.at[own[e], lanes(half, 2 * F)]
            pltpu.make_async_copy(mine[0], arrived, wsems.at[z ^ e, half]).wait()
        part = dot_nt(cbuf[...], wbuf[own[e], :])
        first = first + jnp.sum(part * gains[e : e + 1, :], axis=1, keepdims=True)
        second = second + jnp.sum(part * nbuf[:, own[e]].astype(F32), axis=1, keepdims=True)
        outs[e][:T] = part.astype(outs[e].dtype)
    lane = lax.broadcasted_iota(jnp.int32, (T, 128), 1)
    sums[...] = jnp.where(lane == 0, first, second).T[:8]
    write_rows(outs[3].at[T:], sums[0:2])
    for half in range(2):
        part = dot_nn(nbuf[...], wbuf[:, lanes(half, 2 * F)])
        for a in range(2):
            query[y ^ (2 * half + a)] = part[:, a * F : (a + 1) * F].astype(BF16)


def shape(*dims, dtype=BF16):
    return jax.ShapeDtypeStruct(dims, dtype)


def after(value, dep):
    return lax.optimization_barrier((value, dep))


def merge(a, b, count):
    gap = a[0] - b[0]
    return jnp.stack([0.5 * (a[0] + b[0]), a[1] + b[1] + (0.5 * count) * gap * gap])


def on_device(tokens, gain, w, cot):
    z, y = lax.axis_index("z"), lax.axis_index("y")
    odd = y % 2

    def to_a(s, yy):
        return ((yy >> 1) ^ s, 2 * s + (yy & 1))

    def to_b(s, yy):
        return ((yy >> 1) ^ s, 2 * s + 1 - (yy & 1))

    wa = send(lax.dynamic_slice(w, (odd * F, 0), (F, F)), ("c", "y"), to_a)
    wb = send(lax.dynamic_slice(w, ((1 - odd) * F, 0), (F, F)), ("c", "y"), to_b)
    values = tokens.astype(F32)
    own_mean = jnp.sum(values, axis=1) / F
    centred = values - own_mean[:, None]
    stat = jnp.stack([own_mean, jnp.sum(centred * centred, axis=1)])
    stat = merge(stat, swap(stat, "y", 1), F)
    stat, wa, wb = lax.optimization_barrier((stat, wa, wb))
    stat = merge(stat, swap(stat, "y", 2), 2 * F)

    tok1, tok2 = swap(tokens, "z", 1), swap(tokens, "z", 2)
    tok2, tok1 = after(tok2, tok1)
    tok = [tokens, tok1, tok2, swap(tok2, "z", 1)]

    cot, wa, wb, stat = lax.optimization_barrier((cot, wa, wb, stat))
    cots = lax.all_to_all(jnp.broadcast_to(cot, (4, T, F)), "y", 0, 0, tiled=True)

    w0 = jnp.concatenate([wa, wb], axis=1)
    w1 = swap(w0, "x", 1)
    w3 = swap(w0, "x", 3)
    w_mine = [w0, w1, swap(w0, "x", 2), w3]
    stat, tok1 = after(stat, tok[1])
    packet = jnp.concatenate([stat.reshape(-1), gain])
    other = swap(packet, "z", 1)
    stat = merge(stat, other[: 2 * T].reshape(2, T), 4 * F)
    packet = jnp.concatenate([stat.reshape(-1), gain, other[2 * T :]])
    other2 = swap(packet, "z", 2)
    w_mine, tok[3], other2 = lax.optimization_barrier((w_mine, tok[3], other2))
    w_theirs = [swap(m, "c", 1) for m in w_mine]
    stat = merge(stat, other2[: 2 * T].reshape(2, T), 8 * F)
    gains = [gain, other[2 * T :], other2[2 * T : 2 * T + F], other2[2 * T + F :]]

    width = 16 * F
    inverse = lax.rsqrt(stat[1] / width + 1e-06)[:, None]
    mean = stat[0][:, None]

    def standardize(block):
        return (block.astype(F32) - mean) * inverse

    tok, w_theirs = after(tok, w_theirs)
    normed = [(standardize(b) * g[None, :]).astype(BF16) for b, g in zip(tok, gains)]

    dma = pltpu.SemaphoreType.DMA
    gw = call(
        gw_other_kernel,
        [shape(4, F, 2 * F), shape(4, F, T)],
        [pltpu.VMEM((4, T, F), BF16), pltpu.VMEM((2, T, 2 * F), BF16), dma((8,))],
        1,
        5,
        0,
    )(*normed, cots)
    turned = gw[1]
    gw_theirs = swap(gw[0], "c", 1)

    w_theirs, turned = after(w_theirs, turned)
    *back, query_out, sums = call(
        products_kernel,
        [shape(T, F, dtype=F32), shape(T, F), shape(T, F), shape(T + 16, F)]
        + [shape(4, T, F), shape(8, T, dtype=F32)],
        [
            pltpu.VMEM((4 * F, 4 * F), BF16),
            pltpu.VMEM((T, 4 * F), BF16),
            pltpu.VMEM((T, 4 * F), BF16),
            dma((4, 2)),
            dma((4,)),
            dma((4,)),
        ],
        40_000_000,
        13,
        1,
        15,
    )(*w_mine, *w_theirs, cots, *normed, jnp.stack(gains))
    turned, back = after(turned, back)
    gw_sum = call(
        gw_own_kernel,
        [shape(F, 2 * F, dtype=F32)] + [shape(F, 2 * F)] * 3,
        [pltpu.VMEM((T, 2 * F), BF16), dma((2,))],
        1,
        1,
        2,
    )(cots, turned, gw_theirs)
    gw_parts = [gw_sum[0]] + [swap(gw_sum[e], "x", e) for e in (1, 2, 3)]

    relay = swap(back[3], "z", 1)
    grad1 = swap(back[1], "z", 1)
    relay, gw_parts[0] = after(relay, gw_parts[0])
    query_out, relay = after(query_out, relay)
    message, sums = call(
        message_kernel, [shape(T + 16, F), shape(2, T, dtype=F32)], [], 1, 0, 3
    )(back[2], relay, sums)
    grad2 = swap(message, "z", 2)
    sums = sums + read_rows(grad2[T:])
    grad2 = grad2[:T]
    grad_parts = [back[0], grad1, grad2]


    block = sum(p.astype(F32) for p in gw_parts).astype(BF16)
    block, grad_parts[2] = after(block, grad_parts[2])
    blocks = [block[:, :F], block[:, F:]]

    def home(a):
        return lambda d, cc, yy: (d, yy >> 1, yy ^ (2 * cc + a))

    def away(a):
        return lambda d, cc, yy: (1 - d, yy >> 1, yy ^ (2 * cc + a))

    far = [send(blocks[a], ("dp", "c", "y"), away(a)) for a in (0, 1)]
    near = [send(blocks[a], ("dp", "c", "y"), home(a)) for a in (0, 1)]

    query_parts = lax.all_to_all(query_out, "y", 0, 0, tiled=True)

    query = jnp.sum(query_parts.astype(F32), axis=0).astype(BF16)
    far[1], query = after(far[1], query)
    sums, far = after(sums, far)
    sums = sums + sum(swap(sums, "y", e) for e in (1, 2, 3))
    got_a, got_b = (n.astype(F32) + f.astype(F32) for n, f in zip(near, far))
    even = odd == 0
    grad_w = jnp.concatenate([jnp.where(even, got_a, got_b), jnp.where(even, got_b, got_a)])
    first, second = sums[0][:, None] / width, sums[1][:, None] / width
    grad_hat = sum(p.astype(F32) for p in grad_parts) * gain[None, :]
    token_gradient = ((grad_hat - first - standardize(tokens) * second) * inverse).astype(BF16)
    return query, token_gradient, grad_w


def solution(mesh):
    fine = Mesh(mesh.devices.reshape([SIZES[a] for a in AXES]), AXES)
    rows, cols = ("dp", "x", "c"), ("z", "y")
    in_specs = (P(rows, cols), P(cols), P(("x", "c"), cols), P(rows, cols))
    out_specs = (P(rows, cols), P(rows, cols), P(("x", "c"), cols))
    return jax.shard_map(
        on_device, mesh=fine, in_specs=in_specs, out_specs=out_specs, check_vma=False
    )
```

```python
import functools
import itertools

import jax
import jax.numpy as jnp
from jax import lax
from jax.experimental import pallas as pl
from jax.experimental.pallas import tpu as pltpu
from jax.sharding import Mesh, PartitionSpec as P

AXES = ("dp", "x", "c", "z", "y")
SIZES = dict(dp=2, x=4, c=2, z=4, y=4)
T = 512
F = 384
MIB = 1024 * 1024
F32 = jnp.float32
BF16 = jnp.bfloat16


def send(value, axes, to):
    coords = list(itertools.product(*(range(SIZES[a]) for a in axes)))
    flat = {c: i for i, c in enumerate(coords)}
    perm = [(flat[c], flat[tuple(to(*c))]) for c in coords]
    return lax.ppermute(value, axes if len(axes) > 1 else axes[0], perm)


def swap(value, axis, e):
    return send(value, (axis,), lambda i: (i ^ e,))


def dot_nt(a, b):
    return lax.dot_general(a, b, (((1,), (1,)), ((), ())), preferred_element_type=F32)


def dot_nn(a, b):
    return lax.dot_general(a, b, (((1,), (0,)), ((), ())), preferred_element_type=F32)


def load_all(copies):
    for c in copies:
        c.start()


def lanes(e, width=F):
    return pl.ds(e * width, width)


def call(kernel, out_shape, scratch, cost, n_any, n_vmem, limit=10):
    def outer(*args):
        return pl.pallas_call(
            kernel,
            out_shape=out_shape,
            in_specs=[pl.BlockSpec(memory_space=pl.ANY)] * n_any
            + [pl.BlockSpec(memory_space=pltpu.VMEM)] * n_vmem,
            out_specs=jax.tree.map(lambda _: pl.BlockSpec(memory_space=pltpu.VMEM), out_shape),
            scratch_shapes=scratch,
            compiler_params=pltpu.CompilerParams(vmem_limit_bytes=limit * MIB),
            cost_estimate=pl.CostEstimate(flops=cost, bytes_accessed=cost, transcendentals=0),
        )(*args)

    return outer


def cot_copies(cots, cbuf, sems, first):
    y = lax.axis_index("y")
    return [
        pltpu.make_async_copy(cots.at[y ^ e], cbuf.at[e // 2, :, lanes(e % 2)], sems.at[first + e])
        for e in range(4)
    ]


def gw_other_kernel(*refs):
    normed, cots = refs[0:4], refs[4]
    out, turned = refs[5:7]
    nbuf, cbuf, sems = refs[7:]
    x, c, z = lax.axis_index("x"), lax.axis_index("c"), lax.axis_index("z")
    copies = [pltpu.make_async_copy(normed[e], nbuf.at[z ^ e], sems.at[e]) for e in range(4)]
    copies += cot_copies(cots, cbuf, sems, 4)
    load_all(copies)
    for cp in copies:
        cp.wait()
    for e in range(4):
        row = x ^ e
        nt = nbuf[row].T
        turned[e] = nt
        out[e] = dot_nn(nt, cbuf[1 - c]).astype(BF16)


def gw_own_kernel(*refs):
    cots, turned, other = refs[0:3]
    outs = refs[3:7]
    cbuf, sems = refs[7:]
    c, y = lax.axis_index("c"), lax.axis_index("y")
    copies = [
        pltpu.make_async_copy(cots.at[y ^ (2 * c + a)], cbuf.at[:, lanes(a)], sems.at[a])
        for a in range(2)
    ]
    load_all(copies)
    for cp in copies:
        cp.wait()
    for e in range(4):
        total = dot_nn(turned[e], cbuf[...]) + other[e].astype(F32)
        outs[e][...] = total.astype(outs[e].dtype)


def weight_copies(mine, theirs, wbuf, sems):
    x, c = lax.axis_index("x"), lax.axis_index("c")
    copies = []
    for e in range(4):
        rows = pl.ds(pl.multiple_of((x ^ e) * F, F), F)
        for half, part in ((c, mine[e]), (1 - c, theirs[e])):
            columns = pl.ds(pl.multiple_of(half * 2 * F, 2 * F), 2 * F)
            copies.append(
                pltpu.make_async_copy(part, wbuf.at[rows, columns], sems.at[x ^ e, half])
            )
    return copies


def write_rows(rows, sums):
    hi = sums.astype(BF16)
    rest = sums - hi.astype(F32)
    mid = rest.astype(BF16)
    low = (rest - mid.astype(F32)).astype(BF16)
    parts = jnp.concatenate([hi.astype(F32), mid.astype(F32), low.astype(F32)])
    tail = jnp.concatenate([parts[:, F:], jnp.zeros((6, 2 * F - T), F32)], axis=1)
    rows[...] = jnp.concatenate([parts[:, :F], tail, jnp.zeros((4, F), F32)]).astype(BF16)


def read_rows(rows):
    rows = rows.astype(F32)
    parts = jnp.concatenate([rows[:6], rows[6:12, : T - F]], axis=1)
    return parts[0:2] + parts[2:4] + parts[4:6]


def message_kernel(share, relay, sums, out, total):
    out[:T] = (share[...].astype(F32) + relay[:T].astype(F32)).astype(BF16)
    total[...] = sums[0:2] + read_rows(relay[T:])
    write_rows(out.at[T:], total[...])


def products_kernel(*refs):
    mine, theirs, cots, normed, gains = refs[0:4], refs[4:8], refs[8], refs[9:13], refs[13]
    outs, query, sums = refs[14:18], refs[18], refs[19]
    wbuf, cbuf, nbuf, wsems, csems, nsems = refs[20:]
    y, z = lax.axis_index("y"), lax.axis_index("z")
    columns = [
        pltpu.make_async_copy(cots.at[y ^ e], cbuf.at[:, lanes(e)], csems.at[e]) for e in range(4)
    ]
    load_all(columns)
    load_all(weight_copies(mine, theirs, wbuf, wsems))
    own = [pl.ds(pl.multiple_of((z ^ e) * F, F), F) for e in range(4)]
    features = [
        pltpu.make_async_copy(normed[e], nbuf.at[:, own[e]], nsems.at[e]) for e in range(4)
    ]
    load_all(features)
    for cp in columns + features:
        cp.wait()
    first = jnp.zeros((T, 1), F32)
    second = jnp.zeros((T, 1), F32)
    for e in (3, 2, 1, 0):
        for half in range(2):
            arrived = wbuf.at[own[e], lanes(half, 2 * F)]
            pltpu.make_async_copy(mine[0], arrived, wsems.at[z ^ e, half]).wait()
        part = dot_nt(cbuf[...], wbuf[own[e], :])
        first = first + jnp.sum(part * gains[e : e + 1, :], axis=1, keepdims=True)
        second = second + jnp.sum(part * nbuf[:, own[e]].astype(F32), axis=1, keepdims=True)
        outs[e][:T] = part.astype(outs[e].dtype)
    lane = lax.broadcasted_iota(jnp.int32, (T, 128), 1)
    sums[...] = jnp.where(lane == 0, first, second).T[:8]
    write_rows(outs[3].at[T:], sums[0:2])
    for half in range(2):
        part = dot_nn(nbuf[...], wbuf[:, lanes(half, 2 * F)])
        for a in range(2):
            query[y ^ (2 * half + a)] = part[:, a * F : (a + 1) * F].astype(BF16)


def shape(*dims, dtype=BF16):
    return jax.ShapeDtypeStruct(dims, dtype)


def after(value, dep):
    return lax.optimization_barrier((value, dep))


def merge(a, b, count):
    gap = a[0] - b[0]
    return jnp.stack([0.5 * (a[0] + b[0]), a[1] + b[1] + (0.5 * count) * gap * gap])


def on_device(tokens, gain, w, cot):
    z, y = lax.axis_index("z"), lax.axis_index("y")
    odd = y % 2

    def to_a(s, yy):
        return ((yy >> 1) ^ s, 2 * s + (yy & 1))

    def to_b(s, yy):
        return ((yy >> 1) ^ s, 2 * s + 1 - (yy & 1))

    wa = send(lax.dynamic_slice(w, (odd * F, 0), (F, F)), ("c", "y"), to_a)
    wb = send(lax.dynamic_slice(w, ((1 - odd) * F, 0), (F, F)), ("c", "y"), to_b)
    values = tokens.astype(F32)
    own_mean = jnp.sum(values, axis=1) / F
    centred = values - own_mean[:, None]
    stat = jnp.stack([own_mean, jnp.sum(centred * centred, axis=1)])
    stat = merge(stat, swap(stat, "y", 1), F)
    stat, wa, wb = lax.optimization_barrier((stat, wa, wb))
    stat = merge(stat, swap(stat, "y", 2), 2 * F)

    tok1, tok2 = swap(tokens, "z", 1), swap(tokens, "z", 2)
    tok2, tok1 = after(tok2, tok1)
    tok = [tokens, tok1, tok2, swap(tok2, "z", 1)]

    cot, wa, wb, stat = lax.optimization_barrier((cot, wa, wb, stat))
    cots = lax.all_to_all(jnp.broadcast_to(cot, (4, T, F)), "y", 0, 0, tiled=True)

    w0 = jnp.concatenate([wa, wb], axis=1)
    w1 = swap(w0, "x", 1)
    w3 = swap(w0, "x", 3)
    w_mine = [w0, w1, swap(w0, "x", 2), w3]
    stat, tok1 = after(stat, tok[1])
    packet = jnp.concatenate([stat.reshape(-1), gain])
    other = swap(packet, "z", 1)
    stat = merge(stat, other[: 2 * T].reshape(2, T), 4 * F)
    packet = jnp.concatenate([stat.reshape(-1), gain, other[2 * T :]])
    other2 = swap(packet, "z", 2)
    w_mine, tok[3], other2 = lax.optimization_barrier((w_mine, tok[3], other2))
    w_theirs = [swap(m, "c", 1) for m in w_mine]
    stat = merge(stat, other2[: 2 * T].reshape(2, T), 8 * F)
    gains = [gain, other[2 * T :], other2[2 * T : 2 * T + F], other2[2 * T + F :]]

    width = 16 * F
    inverse = lax.rsqrt(stat[1] / width + 1e-06)[:, None]
    mean = stat[0][:, None]

    def standardize(block):
        return (block.astype(F32) - mean) * inverse

    tok, w_theirs = after(tok, w_theirs)
    normed = [(standardize(b) * g[None, :]).astype(BF16) for b, g in zip(tok, gains)]

    dma = pltpu.SemaphoreType.DMA
    gw = call(
        gw_other_kernel,
        [shape(4, F, 2 * F), shape(4, F, T)],
        [pltpu.VMEM((4, T, F), BF16), pltpu.VMEM((2, T, 2 * F), BF16), dma((8,))],
        1,
        5,
        0,
    )(*normed, cots)
    turned = gw[1]
    gw_theirs = swap(gw[0], "c", 1)

    w_theirs, turned = after(w_theirs, turned)
    *back, query_out, sums = call(
        products_kernel,
        [shape(T, F, dtype=F32), shape(T, F), shape(T, F), shape(T + 16, F)]
        + [shape(4, T, F), shape(8, T, dtype=F32)],
        [
            pltpu.VMEM((4 * F, 4 * F), BF16),
            pltpu.VMEM((T, 4 * F), BF16),
            pltpu.VMEM((T, 4 * F), BF16),
            dma((4, 2)),
            dma((4,)),
            dma((4,)),
        ],
        40_000_000,
        13,
        1,
        15,
    )(*w_mine, *w_theirs, cots, *normed, jnp.stack(gains))
    turned, back = after(turned, back)
    gw_sum = call(
        gw_own_kernel,
        [shape(F, 2 * F, dtype=F32)] + [shape(F, 2 * F)] * 3,
        [pltpu.VMEM((T, 2 * F), BF16), dma((2,))],
        1,
        1,
        2,
    )(cots, turned, gw_theirs)
    gw_parts = [gw_sum[0]] + [swap(gw_sum[e], "x", e) for e in (1, 2, 3)]

    relay = swap(back[3], "z", 1)
    grad1 = swap(back[1], "z", 1)
    relay, gw_parts[0] = after(relay, gw_parts[0])
    query_out, relay = after(query_out, relay)
    message, sums = call(
        message_kernel, [shape(T + 16, F), shape(2, T, dtype=F32)], [], 1, 0, 3
    )(back[2], relay, sums)
    grad2 = swap(message, "z", 2)
    sums = sums + read_rows(grad2[T:])
    grad2 = grad2[:T]
    grad_parts = [back[0], grad1, grad2]


    block = sum(p.astype(F32) for p in gw_parts).astype(BF16)
    block, grad_parts = after(block, grad_parts)
    blocks = [block[:, :F], block[:, F:]]

    def home(a):
        return lambda d, cc, yy: (d, yy >> 1, yy ^ (2 * cc + a))

    def away(a):
        return lambda d, cc, yy: (1 - d, yy >> 1, yy ^ (2 * cc + a))

    far = [send(blocks[a], ("dp", "c", "y"), away(a)) for a in (0, 1)]
    near = [send(blocks[a], ("dp", "c", "y"), home(a)) for a in (0, 1)]

    query_parts = lax.all_to_all(query_out, "y", 0, 0, tiled=True)

    query = jnp.sum(query_parts.astype(F32), axis=0).astype(BF16)
    far[1], query = after(far[1], query)
    sums, near = after(sums, near)
    parts = [swap(sums, "y", e) for e in (1, 2, 3)]
    parts, far = after(parts, far)
    sums = sums + sum(parts)
    got_a, got_b = (n.astype(F32) + f.astype(F32) for n, f in zip(near, far))
    even = odd == 0
    grad_w = jnp.concatenate([jnp.where(even, got_a, got_b), jnp.where(even, got_b, got_a)])
    first, second = sums[0][:, None] / width, sums[1][:, None] / width
    grad_hat = sum(p.astype(F32) for p in grad_parts) * gain[None, :]
    token_gradient = ((grad_hat - first - standardize(tokens) * second) * inverse).astype(BF16)
    return query, token_gradient, grad_w


def solution(mesh):
    fine = Mesh(mesh.devices.reshape([SIZES[a] for a in AXES]), AXES)
    rows, cols = ("dp", "x", "c"), ("z", "y")
    in_specs = (P(rows, cols), P(cols), P(("x", "c"), cols), P(rows, cols))
    out_specs = (P(rows, cols), P(rows, cols), P(("x", "c"), cols))
    return jax.shard_map(
        on_device, mesh=fine, in_specs=in_specs, out_specs=out_specs, check_vma=False
    )
```
